32 devices in a mesh: row: 2 (over y), col: 8 (over z, x), layer: 2 (over core).
Axes of the slice: x: 2, y: 2, z: 4, core: 2. Of those that a mesh axis runs over, the one named last changes fastest.
Arguments:
- s_values: bfloat16 [2, 8, 2, 128, 128], P('row', 'col'), may hold values from -0.5 to 0.5
- s_slots: int32 [2, 8, 2], P('row', 'col'), may hold values from 0 to 16, as said below
- x_values: bfloat16 [4, 2, 8, 1, 128, 128], P(None, 'row', 'col'), may hold values from -6 to 6
- x_slots: int32 [4, 2, 8, 1], P(None, 'row', 'col'), may hold values from 0 to 3, as said below
Outputs:
- product: float32 [2048, 2048], P(('row', 'layer'), 'col')
The draws below stay inside these ranges and needn't reach their ends.
Inputs may be any that keep to these rules, and one draw needn't show every extreme that they name: `s_slots`: within one piece the live values are distinct; the value 8 * 2 marks an empty slot, empty slots follow the live ones, every piece has at least one live slot, and at least one piece has all 2 slots live. `x_slots`: within one piece the 1 positions are distinct.
All inputs are finite; a program needn't handle non-finite values.
Results may differ from the reference program's by a relative error of at most 0.0003.
Values may be sent and summed in bfloat16 or wider, within the bound.
No kernel may reach another device: no remote copies, remote signals or barrier semaphores. Data moves between devices by JAX's collectives and lax.ppermute only.
A program may use at most 64 MiB of HBM per device.

```python
import jax
import jax.numpy as jnp

B = 128
BR = 8
BC = 2
BK = 2
KS = 2
KX = 1
Q = 4
NB = 16
NCB = 16
N_ROW = 2
N_COL = 8


def draw_s_slots(key, part):
    key = jax.random.fold_in(key, 11)
    region = BR * BK
    pieces = N_ROW * N_COL
    keys = jax.random.split(key, pieces + 2)
    orders = jax.vmap(lambda one_key: jax.random.permutation(one_key, region))(keys[:pieces])[:, :KS]
    counts = jax.random.randint(keys[pieces], (pieces,), max(1, KS // 4), KS + 1)
    fullest = jax.random.randint(keys[pieces + 1], (), 0, pieces)
    counts = jnp.where(jnp.arange(pieces) == fullest, KS, counts)
    slots = jnp.where(jnp.arange(KS)[None, :] < counts[:, None], orders, region)
    return slots.reshape(N_ROW, N_COL, KS).astype(jnp.int32)


def draw_x_slots(key, part):
    key = jax.random.fold_in(key, 23)
    region = BK * BC
    pieces = Q * N_ROW * N_COL
    keys = jax.random.split(key, pieces)
    orders = jax.vmap(lambda one_key: jax.random.permutation(one_key, region))(keys)[:, :KX]
    return orders.reshape(Q, N_ROW, N_COL, KX).astype(jnp.int32)


def levels(key, extent, cuts, least, high):
    gain = 1.0
    for axis_at, blocks in cuts:
        heights = jax.random.uniform(jax.random.fold_in(jax.random.fold_in(key, 6), axis_at), (blocks,), jnp.float32, least / len(cuts), high / len(cuts))
        gain = gain * jnp.repeat(jnp.exp(heights), extent[axis_at] // blocks).reshape((-1,) + (1,) * (len(extent) - 1 - axis_at))
    return gain


def gaussian(stream_key, extent, spread, limit, cuts=(), kind=jnp.bfloat16):
    factor_of = levels(stream_key, extent, cuts, -0.22, 0.18) if cuts else 1.0
    result = jax.random.normal(stream_key, extent, jnp.float32) * spread * factor_of
    return jnp.minimum(jnp.maximum(result, -limit), limit).astype(kind)


def setup_inputs(seed: int = 0) -> dict:
    splits = jax.random.split(jax.random.key(seed), 5)
    return {
        "s_values": gaussian(splits[0], (N_ROW, N_COL, KS, B, B), B ** -0.5, 0.5, ((0, 2), (1, 8))),
        "s_slots": draw_s_slots(jax.random.fold_in(splits[4], 71), 0),
        "x_values": gaussian(splits[2], (Q, N_ROW, N_COL, KX, B, B), 1.0, 6.0, ((1, 2), (2, 8))),
        "x_slots": draw_x_slots(jax.random.fold_in(splits[4], 71), 0),
    }


def reference(s_values, s_slots, x_values, x_slots):
    region = BR * BK
    live = s_slots < region
    safe_slots = jnp.where(live, s_slots, 0)
    row_group = jnp.arange(N_ROW, dtype=jnp.int32)[:, None, None]
    piece_index = jnp.arange(N_COL, dtype=jnp.int32)[None, :, None]
    block_rows = row_group * BR + safe_slots // BK
    block_cols = piece_index * BK + safe_slots % BK
    kept = jnp.where(live[..., None, None], s_values.astype(jnp.float32), jnp.float32(0.0))
    s_blocks = jnp.zeros((NB, NB, B, B), jnp.float32).at[block_rows, block_cols].add(kept)
    margin = s_blocks.transpose(0, 2, 1, 3).reshape(NB * B, NB * B).astype(jnp.bfloat16)
    group_index = jnp.arange(Q, dtype=jnp.int32)[:, None, None, None]
    residue = jnp.arange(N_ROW, dtype=jnp.int32)[None, :, None, None]
    column_group = jnp.arange(N_COL, dtype=jnp.int32)[None, None, :, None]
    x_rows = (group_index * N_ROW + residue) * BK + x_slots // BC
    x_cols = column_group * BC + x_slots % BC
    x_blocks = jnp.zeros((NB, NCB, B, B), jnp.float32).at[x_rows, x_cols].add(x_values.astype(jnp.float32))
    density = x_blocks.transpose(0, 2, 1, 3).reshape(NB * B, NCB * B).astype(jnp.bfloat16)
    return jnp.dot(margin, density, preferred_element_type=jnp.float32)
```

```python
import functools

import jax
import jax.numpy as jnp
from jax import lax
from jax.experimental import pallas as pl
from jax.experimental.pallas import tpu as pltpu
from jax.sharding import PartitionSpec as P

BR = 8
BC = 2
TAIL = 16


def pack_kernel(s_ref, s_slots_ref, x_ref, x_slots_ref, s_out, x_out, s_at, x_at, sems):
    block = s_out.shape[-1]
    moves = [(s_slots_ref, s_at), (x_slots_ref, x_at)]
    for ref, out in ((s_ref, s_out), (x_ref, x_out)):
        for at in range(0, ref.shape[0], block):
            rows = pl.ds(at, block)
            moves.append((ref.at[rows], out.at[rows]))
    copies = [pltpu.make_async_copy(*move, sems.at[at]) for at, move in enumerate(moves)]
    for copy in copies:
        copy.start()
    lane = lax.broadcasted_iota(jnp.int32, (TAIL, block), 1)
    for copy, slots, out in zip(copies, (s_at, x_at), (s_out, x_out)):
        copy.wait()
        tail = jnp.zeros(lane.shape, jnp.float32)
        for a in range(slots.shape[0]):
            tail = jnp.where(lane == a, slots[a].astype(jnp.float32), tail)
        out[out.shape[0] - TAIL :] = tail.astype(jnp.bfloat16)
    for copy in copies[2:]:
        copy.wait()


def slots_of(ref, count):
    tail = ref[ref.shape[0] - TAIL :].astype(jnp.float32)
    return [tail[0, a].astype(jnp.int32) for a in range(count)]


def swap_order(n_col):
    far = list(range(n_col - 2, n_col // 2 - 1, -2))
    return far[:1] + list(range(n_col // 2 - 2, 0, -2)) + far[1:]


def add_products(total, pieces, x_all, x_at, slots, inner):
    layer = lax.axis_index("layer")
    block = x_all.shape[-1]
    per_layer = total.shape[0] // block
    zero = jnp.zeros((block, block), jnp.bfloat16)
    s_at = [slots_of(ref, slots) for ref, _ in pieces]
    for first in range(0, len(pieces), 2):
        pair = pieces[first : first + 2]
        x0, x1 = [x_all[piece] for _, piece in pair]
        right = jnp.concatenate(
            [
                jnp.concatenate([x0, zero], axis=1),
                jnp.concatenate([zero, x1], axis=1),
            ],
            axis=0,
        )
        left = jnp.concatenate([ref[: slots * block] for ref, _ in pair], axis=1)
        tiles = jnp.dot(left, right, preferred_element_type=jnp.float32)
        for e, (_, piece) in enumerate(pair):
            x_slot = x_at[piece]
            columns = pl.ds(pl.multiple_of(x_slot % BC * block, block), block)
            for a, s_slot in enumerate(s_at[first + e]):
                at = s_slot // inner - layer * per_layer
                live = (at >= 0) & (at < per_layer) & (s_slot % inner == x_slot // BC)
                rows = pl.ds(pl.multiple_of(jnp.clip(at, 0, per_layer - 1) * block, block), block)
                tile = tiles[a * block : (a + 1) * block, e * block : (e + 1) * block]
                total[rows, columns] += jnp.where(live, tile, 0.0)


def early_kernel(sizes, *refs):
    n_row, n_col, inner, slots, q = sizes
    x_refs, s_refs = refs[:n_row], refs[n_row : n_row + n_col // 2]
    total, x_all, x_at = refs[n_row + n_col // 2 :]
    row, col, layer = lax.axis_index("row"), lax.axis_index("col"), lax.axis_index("layer")
    block = x_all.shape[-1]
    for k, ref in enumerate(x_refs):
        for m, slot in enumerate(slots_of(ref, q)):
            piece = m * n_row + (row ^ k)
            x_all[piece] = ref[m * block : (m + 1) * block]
            x_at[piece] = slot
    total[...] = jnp.zeros_like(total)
    masks = [0] + [mask + layer for mask in swap_order(n_col)]
    pieces = [(ref, col ^ mask) for ref, mask in zip(s_refs, masks)]
    add_products(total, pieces, x_all, x_at, slots, inner)


def final_kernel(sizes, x_at, x_all, total, *refs):
    n_row, n_col, inner, slots, q = sizes
    s_refs, out_ref = refs[:-1], refs[-1]
    col, layer = lax.axis_index("col"), lax.axis_index("layer")
    out_ref[...] = total[...]
    masks = [1] + [mask + 1 - layer for mask in swap_order(n_col)]
    pieces = [(ref, col ^ mask) for ref, mask in zip(s_refs, masks)]
    add_products(out_ref, pieces, x_all, x_at, slots, inner)


def swap(value, n_col, mask, other):
    pairs = []
    for c in range(n_col):
        pairs += [(c * 2, (c ^ mask) * 2), (c * 2 + 1, (c ^ other) * 2 + 1)]
    return lax.ppermute(value, ("col", "layer"), pairs)


def per_device(s_values, s_slots, x_values, x_slots):
    n_row = lax.axis_size("row")
    n_col = lax.axis_size("col")
    n_layer = lax.axis_size("layer")
    block = s_values.shape[-1]
    slots, q = s_values.shape[2], x_values.shape[0]
    arrays = (
        s_values.reshape(slots * block, block),
        s_slots.reshape(slots),
        x_values.reshape(q * block, block),
        x_slots.reshape(q),
    )
    s_piece, x_piece = pl.pallas_call(
        pack_kernel,
        out_shape=(
            pltpu.VMEM((slots * block + TAIL, block), jnp.bfloat16),
            pltpu.VMEM((q * block + TAIL, block), jnp.bfloat16),
        ),
        in_specs=[pl.BlockSpec(memory_space=pltpu.HBM)] * 4,
        out_specs=(pl.BlockSpec(memory_space=pltpu.VMEM),) * 2,
        scratch_shapes=[
            pltpu.SMEM((slots,), jnp.int32),
            pltpu.SMEM((q,), jnp.int32),
            pltpu.SemaphoreType.DMA((2 + slots + q,)),
        ],
        compiler_params=pltpu.CompilerParams(vmem_limit_bytes=4 << 20),
    )(*[pltpu.with_memory_space_constraint(array, pltpu.HBM) for array in arrays])
    order = swap_order(n_col)
    fetched = [swap(s_piece, n_col, mask, mask + 1) for mask in order]
    xs = [x_piece]
    for k in range(1, n_row):
        xs.append(lax.ppermute(x_piece, "row", [(i ^ k, i) for i in range(n_row)]))
    near = swap(s_piece, n_col, 1, 1)
    over = [(i, n_layer - 1 - i) for i in range(n_layer)]
    handed = [lax.ppermute(piece, "layer", over) for piece in fetched]
    smem, vmem = [pl.BlockSpec(memory_space=space) for space in (pltpu.SMEM, pltpu.VMEM)]
    params = pltpu.CompilerParams(vmem_limit_bytes=24 << 20)
    sizes = (n_row, n_col, n_row * BR // n_col, slots, q)
    shape = (BR // n_layer * block, BC * block)
    total, x_all, x_at = pl.pallas_call(
        functools.partial(early_kernel, sizes),
        out_shape=(
            pltpu.VMEM(shape, jnp.float32),
            pltpu.VMEM((q * n_row, block, block), jnp.bfloat16),
            pltpu.SMEM((q * n_row,), jnp.int32),
        ),
        in_specs=[vmem] * (n_row + 1 + len(fetched)),
        out_specs=(vmem, vmem, smem),
        compiler_params=params,
    )(*xs, s_piece, *fetched)
    return pl.pallas_call(
        functools.partial(final_kernel, sizes),
        out_shape=jax.ShapeDtypeStruct(shape, jnp.float32),
        in_specs=[smem] + [vmem] * (3 + len(handed)),
        out_specs=vmem,
        compiler_params=params,
    )(pltpu.with_memory_space_constraint(x_at, pltpu.SMEM), x_all, total, near, *handed)


def solution(mesh):
    placed = (
        P("row", "col", None, None, None),
        P("row", "col", None),
        P(None, "row", "col", None, None, None),
        P(None, "row", "col", None),
    )
    return jax.shard_map(
        per_device,
        mesh=mesh,
        in_specs=placed,
        out_specs=P(("row", "layer"), "col"),
        check_vma=False,
    )
```

```python
import functools

import jax
import jax.numpy as jnp
from jax import lax
from jax.experimental import pallas as pl
from jax.experimental.pallas import tpu as pltpu
from jax.sharding import PartitionSpec as P

BR = 8
BC = 2
TAIL = 16


def pack_kernel(s_ref, s_slots_ref, x_slots_ref, s_out, x_tail_out, s_at, x_at, sems):
    block = s_out.shape[-1]
    moves = [(s_slots_ref, s_at), (x_slots_ref, x_at)]
    for at in range(0, s_ref.shape[0], block):
        rows = pl.ds(at, block)
        moves.append((s_ref.at[rows], s_out.at[rows]))
    copies = [pltpu.make_async_copy(*move, sems.at[at]) for at, move in enumerate(moves)]
    for copy in copies:
        copy.start()
    lane = lax.broadcasted_iota(jnp.int32, (TAIL, block), 1)
    for copy, slots, out in zip(copies, (s_at, x_at), (s_out, x_tail_out)):
        copy.wait()
        tail = jnp.zeros(lane.shape, jnp.float32)
        for a in range(slots.shape[0]):
            tail = jnp.where(lane == a, slots[a].astype(jnp.float32), tail)
        out[out.shape[0] - TAIL :] = tail.astype(jnp.bfloat16)
    for copy in copies[2:]:
        copy.wait()


def join_kernel(x_ref, tail_ref, x_out):
    rows = x_ref.shape[0]
    x_out[:rows] = x_ref[...]
    x_out[rows:] = tail_ref[...]


def slots_of(ref, count):
    tail = ref[ref.shape[0] - TAIL :].astype(jnp.float32)
    return [tail[0, a].astype(jnp.int32) for a in range(count)]


def swap_order(n_col):
    if n_col == 8:
        return [(6, 7), (2, 5), (4, 3)]
    return [(mask, mask + 1) for mask in range(n_col - 2, 0, -2)]


def add_products(total, pieces, x_all, x_at, slots, inner):
    layer = lax.axis_index("layer")
    block = x_all.shape[-1]
    per_layer = total.shape[0] // block
    zero = jnp.zeros((block, block), jnp.bfloat16)
    s_at = [slots_of(ref, slots) for ref, _ in pieces]
    for first in range(0, len(pieces), 2):
        pair = pieces[first : first + 2]
        x0, x1 = [x_all[piece] for _, piece in pair]
        right = jnp.concatenate(
            [
                jnp.concatenate([x0, zero], axis=1),
                jnp.concatenate([zero, x1], axis=1),
            ],
            axis=0,
        )
        left = jnp.concatenate([ref[: slots * block] for ref, _ in pair], axis=1)
        tiles = jnp.dot(left, right, preferred_element_type=jnp.float32)
        for e, (_, piece) in enumerate(pair):
            x_slot = x_at[piece]
            columns = pl.ds(pl.multiple_of(x_slot % BC * block, block), block)
            for a, s_slot in enumerate(s_at[first + e]):
                at = s_slot // inner - layer * per_layer
                live = (at >= 0) & (at < per_layer) & (s_slot % inner == x_slot // BC)
                rows = pl.ds(pl.multiple_of(jnp.clip(at, 0, per_layer - 1) * block, block), block)
                tile = tiles[a * block : (a + 1) * block, e * block : (e + 1) * block]
                total[rows, columns] += jnp.where(live, tile, 0.0)


def early_kernel(sizes, *refs):
    n_row, n_col, inner, slots, q = sizes
    x_refs, s_refs = refs[:n_row], refs[n_row : n_row + n_col // 2]
    total, x_all, x_at = refs[n_row + n_col // 2 :]
    row, col, layer = lax.axis_index("row"), lax.axis_index("col"), lax.axis_index("layer")
    block = x_all.shape[-1]
    for k, ref in enumerate(x_refs):
        for m, slot in enumerate(slots_of(ref, q)):
            piece = m * n_row + (row ^ k)
            x_all[piece] = ref[m * block : (m + 1) * block]
            x_at[piece] = slot
    total[...] = jnp.zeros_like(total)
    masks = [0] + [one + layer * (two - one) for one, two in swap_order(n_col)]
    pieces = [(ref, col ^ mask) for ref, mask in zip(s_refs, masks)]
    add_products(total, pieces, x_all, x_at, slots, inner)


def final_kernel(sizes, x_at, x_all, total, *refs):
    n_row, n_col, inner, slots, q = sizes
    s_refs, out_ref = refs[:-1], refs[-1]
    col, layer = lax.axis_index("col"), lax.axis_index("layer")
    out_ref[...] = total[...]
    masks = [1] + [two + layer * (one - two) for one, two in swap_order(n_col)]
    pieces = [(ref, col ^ mask) for ref, mask in zip(s_refs, masks)]
    add_products(out_ref, pieces, x_all, x_at, slots, inner)


def swap(value, n_col, mask, other):
    pairs = []
    for c in range(n_col):
        pairs += [(c * 2, (c ^ mask) * 2), (c * 2 + 1, (c ^ other) * 2 + 1)]
    return lax.ppermute(value, ("col", "layer"), pairs)


def per_device(s_values, s_slots, x_values, x_slots):
    n_row = lax.axis_size("row")
    n_col = lax.axis_size("col")
    n_layer = lax.axis_size("layer")
    block = s_values.shape[-1]
    slots, q = s_values.shape[2], x_values.shape[0]
    hbm, vmem = [pl.BlockSpec(memory_space=space) for space in (pltpu.HBM, pltpu.VMEM)]
    params = pltpu.CompilerParams(vmem_limit_bytes=4 << 20)
    arrays = s_values.reshape(slots * block, block), s_slots.reshape(slots), x_slots.reshape(q)
    s_piece, x_tail = pl.pallas_call(
        pack_kernel,
        out_shape=(
            pltpu.VMEM((slots * block + TAIL, block), jnp.bfloat16),
            pltpu.VMEM((TAIL, block), jnp.bfloat16),
        ),
        in_specs=[hbm] * len(arrays),
        out_specs=(vmem, vmem),
        scratch_shapes=[
            pltpu.SMEM((slots,), jnp.int32),
            pltpu.SMEM((q,), jnp.int32),
            pltpu.SemaphoreType.DMA((2 + slots,)),
        ],
        compiler_params=params,
        cost_estimate=pl.CostEstimate(flops=1_000_000_000, bytes_accessed=1_000_000, transcendentals=0),
    )(*[pltpu.with_memory_space_constraint(array, pltpu.HBM) for array in arrays])
    x_blocks = pltpu.with_memory_space_constraint(x_values.reshape(q * block, block), pltpu.VMEM)
    x_piece = pl.pallas_call(
        join_kernel,
        out_shape=pltpu.VMEM((q * block + TAIL, block), jnp.bfloat16),
        in_specs=[vmem] * 2,
        out_specs=vmem,
        compiler_params=params,
    )(x_blocks, x_tail)
    order = swap_order(n_col)
    fetched = [swap(s_piece, n_col, *masks) for masks in order]
    xs = [x_piece]
    for k in range(1, n_row):
        xs.append(lax.ppermute(x_piece, "row", [(i ^ k, i) for i in range(n_row)]))
    near = swap(s_piece, n_col, 1, 1)
    over = [(i, n_layer - 1 - i) for i in range(n_layer)]
    handed = [lax.ppermute(piece, "layer", over) for piece in fetched]
    smem, vmem = [pl.BlockSpec(memory_space=space) for space in (pltpu.SMEM, pltpu.VMEM)]
    params = pltpu.CompilerParams(vmem_limit_bytes=24 << 20)
    sizes = (n_row, n_col, n_row * BR // n_col, slots, q)
    shape = (BR // n_layer * block, BC * block)
    total, x_all, x_at = pl.pallas_call(
        functools.partial(early_kernel, sizes),
        out_shape=(
            pltpu.VMEM(shape, jnp.float32),
            pltpu.VMEM((q * n_row, block, block), jnp.bfloat16),
            pltpu.SMEM((q * n_row,), jnp.int32),
        ),
        in_specs=[vmem] * (n_row + 1 + len(fetched)),
        out_specs=(vmem, vmem, smem),
        compiler_params=params,
    )(*xs, s_piece, *fetched)
    return pl.pallas_call(
        functools.partial(final_kernel, sizes),
        out_shape=jax.ShapeDtypeStruct(shape, jnp.float32),
        in_specs=[smem] + [vmem] * (3 + len(handed)),
        out_specs=vmem,
        compiler_params=params,
    )(pltpu.with_memory_space_constraint(x_at, pltpu.SMEM), x_all, total, near, *handed)


def solution(mesh):
    placed = (
        P("row", "col", None, None, None),
        P("row", "col", None),
        P(None, "row", "col", None, None, None),
        P(None, "row", "col", None),
    )
    return jax.shard_map(
        per_device,
        mesh=mesh,
        in_specs=placed,
        out_specs=P(("row", "layer"), "col"),
        check_vma=False,
    )
```

```python
import functools

import jax
import jax.numpy as jnp
from jax import lax
from jax.experimental import pallas as pl
from jax.experimental.pallas import tpu as pltpu
from jax.sharding import PartitionSpec as P

BR = 8
BC = 2
TAIL = 16


def pack_kernel(s_ref, s_slots_ref, x_slots_ref, s_out, x_tail_out, s_at, x_at, sems):
    block = s_out.shape[-1]
    moves = [(s_slots_ref, s_at), (x_slots_ref, x_at)]
    for at in range(0, s_ref.shape[0], block):
        rows = pl.ds(at, block)
        moves.append((s_ref.at[rows], s_out.at[rows]))
    copies = [pltpu.make_async_copy(*move, sems.at[at]) for at, move in enumerate(moves)]
    for copy in copies:
        copy.start()
    lane = lax.broadcasted_iota(jnp.int32, (TAIL, block), 1)
    for copy, slots, out in zip(copies, (s_at, x_at), (s_out, x_tail_out)):
        copy.wait()
        tail = jnp.zeros(lane.shape, jnp.float32)
        for a in range(slots.shape[0]):
            tail = jnp.where(lane == a, slots[a].astype(jnp.float32), tail)
        out[out.shape[0] - TAIL :] = tail.astype(jnp.bfloat16)
    for copy in copies[2:]:
        copy.wait()


def join_kernel(x_ref, tail_ref, x_out):
    rows = x_ref.shape[0]
    x_out[:rows] = x_ref[...]
    x_out[rows:] = tail_ref[...]


def slots_of(ref, count):
    tail = ref[ref.shape[0] - TAIL :].astype(jnp.float32)
    return [tail[0, a].astype(jnp.int32) for a in range(count)]


def swap_order(n_col):
    if n_col == 8:
        return [(6, 7), (2, 4), (5, 3)]
    return [(mask, mask + 1) for mask in range(n_col - 2, 0, -2)]


def add_products(total, pieces, x_all, x_at, slots, inner):
    layer = lax.axis_index("layer")
    block = x_all.shape[-1]
    per_layer = total.shape[0] // block
    zero = jnp.zeros((block, block), jnp.bfloat16)
    s_at = [slots_of(ref, slots) for ref, _ in pieces]
    for first in range(0, len(pieces), 2):
        pair = pieces[first : first + 2]
        x0, x1 = [x_all[piece] for _, piece in pair]
        right = jnp.concatenate(
            [
                jnp.concatenate([x0, zero], axis=1),
                jnp.concatenate([zero, x1], axis=1),
            ],
            axis=0,
        )
        left = jnp.concatenate([ref[: slots * block] for ref, _ in pair], axis=1)
        tiles = jnp.dot(left, right, preferred_element_type=jnp.float32)
        for e, (_, piece) in enumerate(pair):
            x_slot = x_at[piece]
            columns = pl.ds(pl.multiple_of(x_slot % BC * block, block), block)
            for a, s_slot in enumerate(s_at[first + e]):
                at = s_slot // inner - layer * per_layer
                live = (at >= 0) & (at < per_layer) & (s_slot % inner == x_slot // BC)
                rows = pl.ds(pl.multiple_of(jnp.clip(at, 0, per_layer - 1) * block, block), block)
                tile = tiles[a * block : (a + 1) * block, e * block : (e + 1) * block]
                total[rows, columns] += jnp.where(live, tile, 0.0)


def early_kernel(sizes, *refs):
    n_row, n_col, inner, slots, q = sizes
    x_refs, s_refs = refs[:n_row], refs[n_row : n_row + n_col // 2]
    total, x_all, x_at = refs[n_row + n_col // 2 :]
    row, col, layer = lax.axis_index("row"), lax.axis_index("col"), lax.axis_index("layer")
    block = x_all.shape[-1]
    for k, ref in enumerate(x_refs):
        for m, slot in enumerate(slots_of(ref, q)):
            piece = m * n_row + (row ^ k)
            x_all[piece] = ref[m * block : (m + 1) * block]
            x_at[piece] = slot
    total[...] = jnp.zeros_like(total)
    masks = [0] + [one + layer * (two - one) for one, two in swap_order(n_col)]
    pieces = [(ref, col ^ mask) for ref, mask in zip(s_refs, masks)]
    add_products(total, pieces, x_all, x_at, slots, inner)


def final_kernel(sizes, x_at, x_all, total, *refs):
    n_row, n_col, inner, slots, q = sizes
    s_refs, out_ref = refs[:-1], refs[-1]
    col, layer = lax.axis_index("col"), lax.axis_index("layer")
    out_ref[...] = total[...]
    masks = [1] + [two + layer * (one - two) for one, two in swap_order(n_col)]
    pieces = [(ref, col ^ mask) for ref, mask in zip(s_refs, masks)]
    add_products(out_ref, pieces, x_all, x_at, slots, inner)


def swap(value, n_col, mask, other):
    pairs = []
    for c in range(n_col):
        pairs += [(c * 2, (c ^ mask) * 2), (c * 2 + 1, (c ^ other) * 2 + 1)]
    return lax.ppermute(value, ("col", "layer"), pairs)


def per_device(s_values, s_slots, x_values, x_slots):
    n_row = lax.axis_size("row")
    n_col = lax.axis_size("col")
    n_layer = lax.axis_size("layer")
    block = s_values.shape[-1]
    slots, q = s_values.shape[2], x_values.shape[0]
    hbm, vmem = [pl.BlockSpec(memory_space=space) for space in (pltpu.HBM, pltpu.VMEM)]
    params = pltpu.CompilerParams(vmem_limit_bytes=4 << 20)
    arrays = s_values.reshape(slots * block, block), s_slots.reshape(slots), x_slots.reshape(q)
    s_piece, x_tail = pl.pallas_call(
        pack_kernel,
        out_shape=(
            pltpu.VMEM((slots * block + TAIL, block), jnp.bfloat16),
            pltpu.VMEM((TAIL, block), jnp.bfloat16),
        ),
        in_specs=[hbm] * len(arrays),
        out_specs=(vmem, vmem),
        scratch_shapes=[
            pltpu.SMEM((slots,), jnp.int32),
            pltpu.SMEM((q,), jnp.int32),
            pltpu.SemaphoreType.DMA((2 + slots,)),
        ],
        compiler_params=params,
        cost_estimate=pl.CostEstimate(flops=1_000_000_000, bytes_accessed=1_000_000, transcendentals=0),
    )(*[pltpu.with_memory_space_constraint(array, pltpu.HBM) for array in arrays])
    x_blocks = pltpu.with_memory_space_constraint(x_values.reshape(q * block, block), pltpu.VMEM)
    x_piece = pl.pallas_call(
        join_kernel,
        out_shape=pltpu.VMEM((q * block + TAIL, block), jnp.bfloat16),
        in_specs=[vmem] * 2,
        out_specs=vmem,
        compiler_params=params,
    )(x_blocks, x_tail)
    order = swap_order(n_col)
    fetched = [swap(s_piece, n_col, *masks) for masks in order]
    xs = [x_piece]
    for k in range(1, n_row):
        xs.append(lax.ppermute(x_piece, "row", [(i ^ k, i) for i in range(n_row)]))
    near = swap(s_piece, n_col, 1, 1)
    over = [(i, n_layer - 1 - i) for i in range(n_layer)]
    handed = [lax.ppermute(piece, "layer", over) for piece in fetched]
    smem, vmem = [pl.BlockSpec(memory_space=space) for space in (pltpu.SMEM, pltpu.VMEM)]
    params = pltpu.CompilerParams(vmem_limit_bytes=24 << 20)
    sizes = (n_row, n_col, n_row * BR // n_col, slots, q)
    shape = (BR // n_layer * block, BC * block)
    total, x_all, x_at = pl.pallas_call(
        functools.partial(early_kernel, sizes),
        out_shape=(
            pltpu.VMEM(shape, jnp.float32),
            pltpu.VMEM((q * n_row, block, block), jnp.bfloat16),
            pltpu.SMEM((q * n_row,), jnp.int32),
        ),
        in_specs=[vmem] * (n_row + 1 + len(fetched)),
        out_specs=(vmem, vmem, smem),
        compiler_params=params,
    )(*xs, s_piece, *fetched)
    return pl.pallas_call(
        functools.partial(final_kernel, sizes),
        out_shape=jax.ShapeDtypeStruct(shape, jnp.float32),
        in_specs=[smem] + [vmem] * (3 + len(handed)),
        out_specs=vmem,
        compiler_params=params,
    )(pltpu.with_memory_space_constraint(x_at, pltpu.SMEM), x_all, total, near, *handed)


def solution(mesh):
    placed = (
        P("row", "col", None, None, None),
        P("row", "col", None),
        P(None, "row", "col", None, None, None),
        P(None, "row", "col", None),
    )
    return jax.shard_map(
        per_device,
        mesh=mesh,
        in_specs=placed,
        out_specs=P(("row", "layer"), "col"),
        check_vma=False,
    )
```

```python
import functools

import jax
import jax.numpy as jnp
from jax import lax
from jax.experimental import pallas as pl
from jax.experimental.pallas import tpu as pltpu
from jax.sharding import PartitionSpec as P

BR = 8
BC = 2
TAIL = 16


def pack_kernel(s_ref, s_slots_ref, x_slots_ref, s_out, x_tail_out, s_at, x_at, sems):
    block = s_out.shape[-1]
    moves = [(s_slots_ref, s_at), (x_slots_ref, x_at)]
    for at in range(0, s_ref.shape[0], block):
        rows = pl.ds(at, block)
        moves.append((s_ref.at[rows], s_out.at[rows]))
    copies = [pltpu.make_async_copy(*move, sems.at[at]) for at, move in enumerate(moves)]
    for copy in copies:
        copy.start()
    lane = lax.broadcasted_iota(jnp.int32, (TAIL, block), 1)
    for copy, slots, out in zip(copies, (s_at, x_at), (s_out, x_tail_out)):
        copy.wait()
        tail = jnp.zeros(lane.shape, jnp.float32)
        for a in range(slots.shape[0]):
            tail = jnp.where(lane == a, slots[a].astype(jnp.float32), tail)
        out[out.shape[0] - TAIL :] = tail.astype(jnp.bfloat16)
    for copy in copies[2:]:
        copy.wait()


def join_kernel(x_ref, tail_ref, x_out):
    rows = x_ref.shape[0]
    x_out[:rows] = x_ref[...]
    x_out[rows:] = tail_ref[...]


def slots_of(ref, count):
    tail = ref[ref.shape[0] - TAIL :].astype(jnp.float32)
    return [tail[0, a].astype(jnp.int32) for a in range(count)]


def swap_order(n_col):
    if n_col == 8:
        return [(6, 7), (2, 5), (4, 3)]
    return [(mask, mask + 1) for mask in range(n_col - 2, 0, -2)]


def add_products(total, pieces, x_all, x_at, slots, inner):
    layer = lax.axis_index("layer")
    block = x_all.shape[-1]
    per_layer = total.shape[0] // block
    zero = jnp.zeros((block, block), jnp.bfloat16)
    s_at = [slots_of(ref, slots) for ref, _ in pieces]
    for first in range(0, len(pieces), 2):
        pair = pieces[first : first + 2]
        values = [x_all[piece] for _, piece in pair]
        right = values[0]
        if len(pair) == 2:
            right = jnp.concatenate(
                [
                    jnp.concatenate([values[0], zero], axis=1),
                    jnp.concatenate([zero, values[1]], axis=1),
                ],
                axis=0,
            )
        left = jnp.concatenate([ref[: slots * block] for ref, _ in pair], axis=1)
        tiles = jnp.dot(left, right, preferred_element_type=jnp.float32)
        for e, (_, piece) in enumerate(pair):
            x_slot = x_at[piece]
            columns = pl.ds(pl.multiple_of(x_slot % BC * block, block), block)
            for a, s_slot in enumerate(s_at[first + e]):
                at = s_slot // inner - layer * per_layer
                live = (at >= 0) & (at < per_layer) & (s_slot % inner == x_slot // BC)
                rows = pl.ds(pl.multiple_of(jnp.clip(at, 0, per_layer - 1) * block, block), block)
                tile = tiles[a * block : (a + 1) * block, e * block : (e + 1) * block]
                total[rows, columns] += jnp.where(live, tile, 0.0)


def lay_out(sizes, k, ref, x_all):
    n_row, _, _, _, q = sizes
    block = x_all.shape[-1]
    for m in range(q):
        x_all[m * n_row + (lax.axis_index("row") ^ k)] = ref[m * block : (m + 1) * block]


def prepare_kernel(sizes, x_ref, total, x_all):
    total[...] = jnp.zeros_like(total)
    lay_out(sizes, 0, x_ref, x_all)


def early_kernel(sizes, _, __, *refs):
    n_row, n_col, inner, slots, q = sizes
    x_refs, s_refs = refs[:n_row], refs[n_row:-3]
    total, x_all, x_at = refs[-3:]
    row, col, layer = lax.axis_index("row"), lax.axis_index("col"), lax.axis_index("layer")
    for k, ref in enumerate(x_refs):
        if k:
            lay_out(sizes, k, ref, x_all)
        for m, slot in enumerate(slots_of(ref, q)):
            x_at[m * n_row + (row ^ k)] = slot
    masks = [0] + [one + layer * (two - one) for one, two in swap_order(n_col)]
    pieces = [(ref, col ^ mask) for ref, mask in zip(s_refs, masks)]
    add_products(total, pieces, x_all, x_at, slots, inner)


def final_kernel(sizes, x_at, x_all, total, *refs):
    n_row, n_col, inner, slots, q = sizes
    s_refs, out_ref = refs[:-1], refs[-1]
    col, layer = lax.axis_index("col"), lax.axis_index("layer")
    out_ref[...] = total[...]
    masks = [1] + [two + layer * (one - two) for one, two in swap_order(n_col)]
    pieces = [(ref, col ^ mask) for ref, mask in zip(s_refs, masks)]
    add_products(out_ref, pieces, x_all, x_at, slots, inner)


def swap(value, n_col, mask, other):
    pairs = []
    for c in range(n_col):
        pairs += [(c * 2, (c ^ mask) * 2), (c * 2 + 1, (c ^ other) * 2 + 1)]
    return lax.ppermute(value, ("col", "layer"), pairs)


def per_device(s_values, s_slots, x_values, x_slots):
    n_row = lax.axis_size("row")
    n_col = lax.axis_size("col")
    n_layer = lax.axis_size("layer")
    block = s_values.shape[-1]
    slots, q = s_values.shape[2], x_values.shape[0]
    hbm, vmem = [pl.BlockSpec(memory_space=space) for space in (pltpu.HBM, pltpu.VMEM)]
    params = pltpu.CompilerParams(vmem_limit_bytes=4 << 20)
    arrays = s_values.reshape(slots * block, block), s_slots.reshape(slots), x_slots.reshape(q)
    s_piece, x_tail = pl.pallas_call(
        pack_kernel,
        out_shape=(
            pltpu.VMEM((slots * block + TAIL, block), jnp.bfloat16),
            pltpu.VMEM((TAIL, block), jnp.bfloat16),
        ),
        in_specs=[hbm] * len(arrays),
        out_specs=(vmem, vmem),
        scratch_shapes=[
            pltpu.SMEM((slots,), jnp.int32),
            pltpu.SMEM((q,), jnp.int32),
            pltpu.SemaphoreType.DMA((2 + slots,)),
        ],
        compiler_params=params,
        cost_estimate=pl.CostEstimate(flops=1_000_000_000, bytes_accessed=1_000_000, transcendentals=0),
    )(*[pltpu.with_memory_space_constraint(array, pltpu.HBM) for array in arrays])
    x_blocks = pltpu.with_memory_space_constraint(x_values.reshape(q * block, block), pltpu.VMEM)
    x_piece = pl.pallas_call(
        join_kernel,
        out_shape=pltpu.VMEM((q * block + TAIL, block), jnp.bfloat16),
        in_specs=[vmem] * 2,
        out_specs=vmem,
        compiler_params=params,
    )(x_blocks, x_tail)
    order = swap_order(n_col)
    fetched = [swap(s_piece, n_col, *masks) for masks in order]
    xs = [x_piece]
    for k in range(1, n_row):
        xs.append(lax.ppermute(x_piece, "row", [(i ^ k, i) for i in range(n_row)]))
    near = swap(s_piece, n_col, 1, 1)
    over = [(i, n_layer - 1 - i) for i in range(n_layer)]
    handed = [lax.ppermute(piece, "layer", over) for piece in fetched]
    smem, vmem = [pl.BlockSpec(memory_space=space) for space in (pltpu.SMEM, pltpu.VMEM)]
    params = pltpu.CompilerParams(vmem_limit_bytes=24 << 20)
    sizes = (n_row, n_col, n_row * BR // n_col, slots, q)
    shape = (BR // n_layer * block, BC * block)
    prepared = (
        pltpu.VMEM(shape, jnp.float32),
        pltpu.VMEM((q * n_row, block, block), jnp.bfloat16),
    )
    started = pl.pallas_call(
        functools.partial(prepare_kernel, sizes),
        out_shape=prepared,
        in_specs=[vmem],
        out_specs=(vmem, vmem),
        compiler_params=params,
    )(x_piece)
    total, x_all, x_at = pl.pallas_call(
        functools.partial(early_kernel, sizes),
        out_shape=(*prepared, pltpu.SMEM((q * n_row,), jnp.int32)),
        in_specs=[vmem] * (n_row + 3 + len(fetched)),
        out_specs=(vmem, vmem, smem),
        input_output_aliases={0: 0, 1: 1},
        compiler_params=params,
    )(
        *[pltpu.with_memory_space_constraint(array, pltpu.VMEM) for array in started],
        *xs,
        s_piece,
        *fetched,
    )
    return pl.pallas_call(
        functools.partial(final_kernel, sizes),
        out_shape=jax.ShapeDtypeStruct(shape, jnp.float32),
        in_specs=[smem] + [vmem] * (3 + len(handed)),
        out_specs=vmem,
        compiler_params=params,
    )(pltpu.with_memory_space_constraint(x_at, pltpu.SMEM), x_all, total, near, *handed)


def solution(mesh):
    placed = (
        P("row", "col", None, None, None),
        P("row", "col", None),
        P(None, "row", "col", None, None, None),
        P(None, "row", "col", None),
    )
    return jax.shard_map(
        per_device,
        mesh=mesh,
        in_specs=placed,
        out_specs=P(("row", "layer"), "col"),
        check_vma=False,
    )
```
